128 devices in a mesh: pb: 8 (over y, x_hi), kv: 16 (over z, x_lo, core).
Axes of the slice: x: 4 (x_hi: 2, x_lo: 2; x = x_hi * 2 + x_lo), y: 4, z: 4, core: 2. Of those that a mesh axis runs over, the one named last changes fastest.
Arguments:
- query_proj: bfloat16 [8192, 1024], P(('pb', 'kv')), may hold values from -6 to 6
- key_proj: bfloat16 [8192, 1024], P(('kv', 'pb')), may hold values from -8 to 8
- value_proj: bfloat16 [8192, 1024], P(('kv', 'pb')), may hold values from -6 to 6
- grad_attn: bfloat16 [8192, 1024], P(('pb', 'kv')), may hold values from -384 to 384
Outputs:
- query_grad: float32 [8192, 1024], P(('pb', 'kv'))
- key_grad: float32 [8192, 1024], P(('kv', 'pb'))
- value_grad: float32 [8192, 1024], P(('kv', 'pb'))
The draws below stay inside these ranges and needn't reach their ends.
All inputs are finite; a program needn't handle non-finite values.
Results may differ from the reference program's by a relative error of at most 0.0095.
Values may be sent and summed in bfloat16 or wider, within the bound.
No kernel may reach another device: no remote copies, remote signals or barrier semaphores. Data moves between devices by JAX's collectives and lax.ppermute only.
A program may use at most 128 MiB of HBM per device.

```python
import jax
import jax.numpy as jnp
from jax import lax

HEADS = 16
HEAD_DIM = 64
FEAT = 1024
QUERIES = 8192
TOKENS = 8192


def draw_query_proj(key, part):
    key = jax.random.fold_in(key, 1)
    first = jax.random.fold_in(key, 0)
    base = jnp.clip(jax.random.normal(first, (QUERIES, FEAT), jnp.float32), -5.0, 5.0)
    return base.astype(jnp.bfloat16)


def draw_key_proj(key, part):
    key = jax.random.fold_in(key, 2)
    first = jax.random.fold_in(key, 0)
    rows = jnp.arange(TOKENS, dtype=jnp.int32)
    ramp = 0.55 + rows.astype(jnp.float32) / TOKENS
    base = jnp.clip(jax.random.normal(first, (TOKENS, FEAT), jnp.float32), -5.0, 5.0) * ramp[:, None]
    return base.astype(jnp.bfloat16)


def steps_of(key, extent, pieces, least, largest):
    factor_of = 1.0
    for position, blocks in pieces:
        steps = jax.random.uniform(jax.random.fold_in(jax.random.fold_in(key, 6), position), (blocks,), jnp.float32, least / len(pieces), largest / len(pieces))
        factor_of = factor_of * jnp.repeat(jnp.exp(steps), extent[position] // blocks).reshape((-1,) + (1,) * (len(extent) - 1 - position))
    return factor_of


def bell_draw(stream_key, shape, deviation, most, cuts=(), held_as=jnp.bfloat16):
    loudness = steps_of(stream_key, shape, cuts, -0.22, 0.18) if cuts else 1.0
    values = jax.random.normal(stream_key, shape, jnp.float32) * deviation * loudness
    return jnp.minimum(jnp.maximum(values, -most), most).astype(held_as)


def setup_inputs(seed: int = 0) -> dict:
    arg_keys = jax.random.split(jax.random.key(seed), 5)
    query_proj = draw_query_proj(jax.random.fold_in(arg_keys[4], 71), 0)
    key_proj = draw_key_proj(jax.random.fold_in(arg_keys[4], 71), 0)
    value_proj = bell_draw(arg_keys[2], (TOKENS, FEAT), 1.0, 6.0, ((0, 128),))
    grad_attn = bell_draw(arg_keys[3], (QUERIES, FEAT), 64.0, 384.0, ((0, 128),))
    return dict(query_proj=query_proj, key_proj=key_proj, value_proj=value_proj, grad_attn=grad_attn)


def reference(query_proj, key_proj, value_proj, grad_attn):
    scale = HEAD_DIM ** -0.5
    row_size = 2048 if QUERIES % 2048 == 0 else QUERIES

    def one_head(head):
        start = (head * HEAD_DIM).astype(jnp.int32)
        query_head = lax.dynamic_slice_in_dim(query_proj, start, HEAD_DIM, 1)
        key_head = lax.dynamic_slice_in_dim(key_proj, start, HEAD_DIM, 1)
        value_head = lax.dynamic_slice_in_dim(value_proj, start, HEAD_DIM, 1)
        grad_head = lax.dynamic_slice_in_dim(grad_attn, start, HEAD_DIM, 1)
        query_blocks = query_head.reshape(QUERIES // row_size, row_size, HEAD_DIM)
        grad_blocks = grad_head.reshape(QUERIES // row_size, row_size, HEAD_DIM)

        def step(carry, inputs):
            current, grad_now = inputs
            scores = jnp.dot(current, key_head.T, preferred_element_type=jnp.float32) * scale
            peak = jnp.max(scores, axis=1, keepdims=True)
            expo = jnp.exp(scores - peak)
            total = jnp.sum(expo, axis=1, keepdims=True)
            probs = expo / total
            slopes = jnp.dot(grad_now, value_head.T, preferred_element_type=jnp.float32)
            delta = jnp.sum(probs * slopes, axis=1, keepdims=True)
            weights = (probs * (slopes - delta)).astype(jnp.bfloat16)
            query_part = jnp.dot(weights, key_head, preferred_element_type=jnp.float32) * scale
            key_sum = carry[0] + jnp.dot(weights.T, current, preferred_element_type=jnp.float32) * scale
            value_sum = carry[1] + jnp.dot(probs.astype(jnp.bfloat16).T, grad_now, preferred_element_type=jnp.float32)
            return (key_sum, value_sum), query_part

        zeros = jnp.zeros((TOKENS, HEAD_DIM), jnp.float32)
        (key_sum, value_sum), query_parts = lax.scan(step, (zeros, zeros), (query_blocks, grad_blocks))
        return query_parts.reshape(QUERIES, HEAD_DIM), key_sum, value_sum

    query_all, key_all, value_all = lax.map(one_head, jnp.arange(HEADS, dtype=jnp.int32))
    query_grad = jnp.transpose(query_all, (1, 0, 2)).reshape(QUERIES, FEAT)
    key_grad = jnp.transpose(key_all, (1, 0, 2)).reshape(TOKENS, FEAT)
    value_grad = jnp.transpose(value_all, (1, 0, 2)).reshape(TOKENS, FEAT)
    return query_grad, key_grad, value_grad
```

```python
import functools

import jax
import jax.numpy as jnp
from jax import lax
from jax.experimental import pallas as pl
from jax.experimental.pallas import tpu as pltpu
from jax.sharding import Mesh, PartitionSpec as P

HEADS = 16
HEAD_DIM = 64
LOG2E = 1.4426950408889634
NN = (((1,), (0,)), ((), ()))
CHIPS = ("xh", "z", "xl")
QUERY_BLOCK = 512
TOKEN_CHUNK = 512


def dot(left, right):
    return lax.dot_general(left, right, NN, preferred_element_type=jnp.float32)


def head_kernel(qg_ref, kv_ref, dq_ref, dkv_ref, e_ref, slope_ref, peak_ref, kt_ref):
    step = pl.program_id(0)
    count = qg_ref.shape[0]
    tokens = kv_ref.shape[0]
    chunk = TOKEN_CHUNK

    def rows_of(i):
        return pl.ds(pl.multiple_of(i * chunk, chunk), chunk)

    @pl.when(step == 0)
    def _():
        dkv_ref[...] = jnp.zeros_like(dkv_ref)

        def turn(i, carry):
            block = kv_ref[rows_of(i), :].astype(jnp.float32)
            kt_ref[:, rows_of(i)] = block.T[:HEAD_DIM].astype(jnp.bfloat16)
            return carry

        lax.fori_loop(0, tokens // chunk, turn, 0)

    qg = qg_ref[...]
    lane = lax.broadcasted_iota(jnp.int32, qg.shape, 1)
    zero = jnp.zeros_like(qg)
    query = jnp.where(lane < HEAD_DIM, qg * jnp.bfloat16(HEAD_DIM**-0.5), zero)
    grad = jnp.where(lane < HEAD_DIM, zero, qg)
    query_t = query.astype(jnp.float32).T.astype(jnp.bfloat16)
    grad_t = grad.astype(jnp.float32).T.astype(jnp.bfloat16)
    both = jnp.concatenate([query, grad], axis=0)

    def forward(i, carry):
        peak, total, delta = carry
        kv = kv_ref[rows_of(i), :]
        scores = dot(kv, query_t)
        new = jnp.maximum(peak, jnp.max(scores, axis=0, keepdims=True))
        shrink = jnp.exp2((peak - new) * LOG2E)
        e = jnp.exp2((scores - new) * LOG2E)
        e_ref[rows_of(i), :] = e
        slopes = dot(kv, grad_t)
        slope_ref[rows_of(i), :] = slopes
        peak_ref[pl.ds(i, 1), :] = new
        total = total * shrink + jnp.sum(e, axis=0, keepdims=True)
        delta = delta * shrink + jnp.sum(e * slopes, axis=0, keepdims=True)
        return new, total, delta

    none = jnp.zeros((1, count), jnp.float32)
    peak, total, delta = lax.fori_loop(
        0, tokens // chunk, forward, (jnp.full((1, count), -jnp.inf, jnp.float32), none, none)
    )
    inverse = 1.0 / total
    delta = delta * inverse

    def backward(i, dq_t):
        factor = jnp.exp2((peak_ref[pl.ds(i, 1), :] - peak) * LOG2E) * inverse
        probs = e_ref[rows_of(i), :] * factor
        weights = (probs * (slope_ref[rows_of(i), :] - delta)).astype(jnp.bfloat16)
        pair = jnp.concatenate([weights, probs.astype(jnp.bfloat16)], axis=1)
        dkv_ref[rows_of(i), :] += dot(pair, both)
        return dq_t + dot(kt_ref[:, rows_of(i)], weights)

    dq_t = lax.fori_loop(
        0, tokens // chunk, backward, jnp.zeros((HEAD_DIM, count), jnp.float32)
    )
    dq_ref[...] = dq_t.T * HEAD_DIM**-0.5


def attend_backward(qg, kv):
    queries, tokens = qg.shape[0], kv.shape[0]
    wide = 2 * HEAD_DIM
    return pl.pallas_call(
        head_kernel,
        grid=(queries // QUERY_BLOCK,),
        in_specs=[
            pl.BlockSpec((QUERY_BLOCK, wide), lambda i: (i, 0)),
            pl.BlockSpec((tokens, wide), lambda i: (0, 0)),
        ],
        out_specs=[
            pl.BlockSpec((QUERY_BLOCK, HEAD_DIM), lambda i: (i, 0)),
            pl.BlockSpec((tokens, wide), lambda i: (0, 0)),
        ],
        out_shape=[
            jax.ShapeDtypeStruct((queries, HEAD_DIM), jnp.float32),
            jax.ShapeDtypeStruct((tokens, wide), jnp.float32),
        ],
        scratch_shapes=[
            pltpu.VMEM((tokens, QUERY_BLOCK), jnp.float32),
            pltpu.VMEM((tokens, QUERY_BLOCK), jnp.float32),
            pltpu.VMEM((tokens // TOKEN_CHUNK, QUERY_BLOCK), jnp.float32),
            pltpu.VMEM((HEAD_DIM, tokens), jnp.bfloat16),
        ],
        compiler_params=pltpu.CompilerParams(
            vmem_limit_bytes=60 * 2**20, dimension_semantics=("arbitrary",)
        ),
    )(qg, kv)


def ring(step, size):
    return [(i, (i + step) % size) for i in range(size)]


def per_device(query_proj, key_proj, value_proj, grad_attn, *, around):
    rows = query_proj.shape[0]
    low = jnp.bfloat16
    packed = jnp.concatenate(
        [
            a.reshape(rows, HEADS, HEAD_DIM)
            for a in (query_proj, grad_attn, key_proj, value_proj)
        ],
        axis=2,
    ).transpose(1, 0, 2)
    mine = lax.all_to_all(packed, CHIPS, 0, 0, tiled=True).reshape(
        HEADS * rows, 4 * HEAD_DIM
    )
    qg, kv = mine[:, : 2 * HEAD_DIM], mine[:, 2 * HEAD_DIM :]
    half = jnp.concatenate(
        [kv] + [lax.ppermute(kv, "y", ring(k, around)) for k in range(1, around)], axis=0
    )
    swap = [(0, 1), (1, 0)]
    tokens = jnp.concatenate([half, lax.ppermute(half, "core", swap)], axis=0)
    dq, dkv = attend_backward(qg, tokens)
    own, other = dkv[: half.shape[0]], dkv[half.shape[0] :]
    own = (own + lax.ppermute(other, "core", swap)).reshape(around, *kv.shape)
    total = own[0]
    for k in range(1, around):
        total = total + lax.ppermute(own[k].astype(low), "y", ring(-k, around)).astype(
            jnp.float32
        )
    out = jnp.concatenate([dq, total], axis=1).astype(low).reshape(HEADS, rows, 3 * HEAD_DIM)
    out = lax.all_to_all(out, CHIPS, 0, 0, tiled=True).transpose(1, 0, 2).astype(jnp.float32)
    return tuple(
        out[:, :, k * HEAD_DIM : (k + 1) * HEAD_DIM].reshape(rows, HEADS * HEAD_DIM)
        for k in range(3)
    )


def solution(mesh):
    fine = Mesh(
        mesh.devices.reshape(4, 2, 4, 2, 2), ("y", "xh", "z", "xl", "core")
    )
    queries = P(("y", "xh", "z", "xl", "core"), None)
    tokens = P(("z", "xl", "core", "y", "xh"), None)
    return jax.shard_map(
        functools.partial(per_device, around=4),
        mesh=fine,
        in_specs=(queries, tokens, tokens, queries),
        out_specs=(queries, tokens, tokens),
        check_vma=False,
    )
```

```python
import functools

import jax
import jax.numpy as jnp
from jax import lax
from jax.experimental import pallas as pl
from jax.experimental.pallas import tpu as pltpu
from jax.sharding import Mesh, PartitionSpec as P

HEADS = 16
HEAD_DIM = 64
WIDE = 2 * HEAD_DIM
LOG2E = 1.4426950408889634
NN = (((1,), (0,)), ((), ()))
CHIPS = ("xh", "z", "xl")
QUERY_BLOCK = 512
GROUP = 2048
PARAMS = pltpu.CompilerParams(
    vmem_limit_bytes=60 * 2**20, dimension_semantics=("arbitrary",)
)


def dot(left, right):
    return lax.dot_general(left, right, NN, preferred_element_type=jnp.float32)


def fold(values, op):
    return op(values.reshape(values.shape[0] // 8, 8, values.shape[1]), axis=0)


def over_rows(start, rows, step, unroll, body, carry):
    def iteration(i, carry):
        for j in range(unroll // step):
            first = start + i * unroll + j * step
            carry = body(pl.ds(pl.multiple_of(first, step), step), carry)
        return carry

    return lax.fori_loop(0, rows // unroll, iteration, carry)


def head_kernel(
    qg_ref, kv_ref, dq_ref, own_ref, other_ref, e_ref, slope_ref, kt_ref, sum_ref, dqt_ref, stat_ref
):
    step = pl.program_id(0)
    queries = qg_ref.shape[0]
    tokens = kv_ref.shape[0]
    blocks = queries // QUERY_BLOCK
    low = jnp.bfloat16

    def operands(block):
        qg = qg_ref[pl.ds(block * QUERY_BLOCK, QUERY_BLOCK), :]
        lane = lax.broadcasted_iota(jnp.int32, qg.shape, 1)
        zero = jnp.zeros_like(qg)
        query = jnp.where(lane < HEAD_DIM, qg * low(HEAD_DIM**-0.5), zero)
        return query, jnp.where(lane < HEAD_DIM, zero, qg)

    def statistics(block, query, grad):
        query_t, grad_t = query.T, grad.T

        def scores_of(rows, peak):
            kv = kv_ref[rows, :]
            scores = dot(kv, query_t)
            e_ref[rows, :] = scores
            if block == 0:
                kt_ref[:, rows] = kv.T[:HEAD_DIM]
            return jnp.maximum(peak, fold(scores, jnp.max))

        peak = over_rows(
            0, tokens, 512, tokens, scores_of, jnp.full((8, QUERY_BLOCK), -jnp.inf, jnp.float32)
        )
        peak = jnp.max(peak, axis=0, keepdims=True) * LOG2E

        def sums_of(rows, carry):
            total, delta = carry
            slopes = dot(kv_ref[rows, :], grad_t)
            slope_ref[rows, :] = slopes
            e = jnp.exp2(e_ref[rows, :] * LOG2E - peak)
            e_ref[rows, :] = e
            return total + fold(e, jnp.sum), delta + fold(e * slopes, jnp.sum)

        none = jnp.zeros((8, QUERY_BLOCK), jnp.float32)
        total, delta = over_rows(0, tokens, 512, GROUP, sums_of, (none, none))
        inverse = 1.0 / jnp.sum(total, axis=0, keepdims=True)
        return inverse, jnp.sum(delta, axis=0, keepdims=True) * inverse

    def gradients(first, rows, query, grad, inverse, delta, put, dq_t):
        both = jnp.concatenate([query, grad], axis=0)

        def part(rows, dq_t):
            probs = e_ref[rows, :] * inverse
            weights = (probs * (slope_ref[rows, :] - delta)).astype(low)
            pair = jnp.concatenate([weights, probs.astype(low)], axis=1)
            put(rows, dot(pair, both))
            return dq_t + dot(kt_ref[:, rows], weights)

        return over_rows(first, rows, 256, GROUP, part, dq_t)

    def put_dq(block, dq_t):
        dq = dq_t.T * HEAD_DIM**-0.5
        for i in range(QUERY_BLOCK // 64):
            rows = dq[i * 64 : (i + 1) * 64]
            dq_ref[block * (QUERY_BLOCK // 64) + i] = jnp.concatenate(
                [rows[:32], rows[32:]], axis=1
            ).astype(low)

    @pl.when(step == 0)
    def _():
        for block in range(blocks):
            query, grad = operands(block)
            inverse, delta = statistics(block, query, grad)
            if block == blocks - 1:
                stat_ref[0:1, :] = inverse
                stat_ref[1:2, :] = delta
                break

            def put(rows, part):
                sum_ref[rows, :] = part if block == 0 else sum_ref[rows, :] + part

            dq_t = gradients(
                0, tokens, query, grad, inverse, delta, put, jnp.zeros(dqt_ref.shape, jnp.float32)
            )
            put_dq(block, dq_t)
        dqt_ref[...] = jnp.zeros_like(dqt_ref)

    half = tokens // 2
    query, grad = operands(blocks - 1)

    def last(first, out_ref):
        def put(rows, part):
            out_ref[pl.ds(pl.multiple_of(rows.start - first, 256), 256), :] = sum_ref[rows, :] + part

        dqt_ref[...] = gradients(
            first, GROUP, query, grad, stat_ref[0:1, :], stat_ref[1:2, :], put, dqt_ref[...]
        )

    per_half = half // GROUP

    @pl.when(step < per_half)
    def _():
        last(half + step * GROUP, other_ref)

    @pl.when(step >= per_half)
    def _():
        last((step - per_half) * GROUP, own_ref)

    @pl.when(step == 2 * per_half - 1)
    def _():
        put_dq(blocks - 1, dqt_ref[...])


def attend_backward(qg, kv):
    queries, tokens = qg.shape[0], kv.shape[0]
    half = tokens // 2
    per_half = half // GROUP
    return pl.pallas_call(
        head_kernel,
        grid=(2 * per_half,),
        in_specs=[
            pl.BlockSpec((queries, WIDE), lambda i: (0, 0)),
            pl.BlockSpec((tokens, WIDE), lambda i: (0, 0)),
        ],
        out_specs=[
            pl.BlockSpec((queries // 64, 32, WIDE), lambda i: (0, 0, 0)),
            pl.BlockSpec((GROUP, WIDE), lambda i: (jnp.maximum(i - per_half, 0), 0)),
            pl.BlockSpec((GROUP, WIDE), lambda i: (jnp.minimum(i, per_half - 1), 0)),
        ],
        out_shape=[
            jax.ShapeDtypeStruct((queries // 64, 32, WIDE), jnp.bfloat16),
            jax.ShapeDtypeStruct((half, WIDE), jnp.float32),
            jax.ShapeDtypeStruct((half, WIDE), jnp.float32),
        ],
        scratch_shapes=[
            pltpu.VMEM((tokens, QUERY_BLOCK), jnp.float32),
            pltpu.VMEM((tokens, QUERY_BLOCK), jnp.float32),
            pltpu.VMEM((HEAD_DIM, tokens), jnp.bfloat16),
            pltpu.VMEM((tokens, WIDE), jnp.float32),
            pltpu.VMEM((HEAD_DIM, QUERY_BLOCK), jnp.float32),
            pltpu.VMEM((8, QUERY_BLOCK), jnp.float32),
        ],
        compiler_params=PARAMS,
    )(qg, kv)


def whole():
    return pl.BlockSpec(memory_space=pltpu.VMEM)


def pack_kernel(left_ref, right_ref, out_ref):
    for head in range(HEADS):
        columns = slice(head * HEAD_DIM, (head + 1) * HEAD_DIM)
        out_ref[head] = jnp.concatenate([left_ref[:, columns], right_ref[:, columns]], axis=1)


def pack(left, right):
    rows = left.shape[0]
    return pl.pallas_call(
        pack_kernel,
        in_specs=[whole(), whole()],
        out_specs=whole(),
        out_shape=jax.ShapeDtypeStruct((HEADS, rows, WIDE), left.dtype),
    )(left, right)


def unpack_kernel(in_ref, dq_ref, dk_ref, dv_ref):
    for pair in range(HEADS // 2):
        one, two = (in_ref[2 * pair + i].astype(jnp.float32) for i in range(2))
        columns = slice(pair * WIDE, (pair + 1) * WIDE)
        dq_ref[:32, columns] = jnp.concatenate([one[:32, :HEAD_DIM], two[:32, :HEAD_DIM]], axis=1)
        dq_ref[32:, columns] = jnp.concatenate([one[:32, HEAD_DIM:], two[:32, HEAD_DIM:]], axis=1)
        dk_ref[:, columns] = jnp.concatenate([one[32:, :HEAD_DIM], two[32:, :HEAD_DIM]], axis=1)
        dv_ref[:, columns] = jnp.concatenate([one[32:, HEAD_DIM:], two[32:, HEAD_DIM:]], axis=1)


def unpack(mine):
    out = jax.ShapeDtypeStruct((64, HEADS * HEAD_DIM), jnp.float32)
    return pl.pallas_call(
        unpack_kernel, in_specs=[whole()], out_specs=[whole()] * 3, out_shape=[out] * 3
    )(mine)


def ring(step, size):
    return [(i, (i + step) % size) for i in range(size)]


def per_device(query_proj, key_proj, value_proj, grad_attn, *, around):
    low = jnp.bfloat16

    def spread(packed):
        return lax.all_to_all(packed, CHIPS, 0, 0, tiled=True)

    kv = spread(pack(key_proj, value_proj)).reshape(-1, WIDE)
    parts = [kv] + [lax.ppermute(kv, "y", ring(k, around)) for k in range(1, around)]
    qg = spread(pack(query_proj, grad_attn)).reshape(-1, WIDE)
    *parts, qg = lax.optimization_barrier((*parts, qg))
    half = jnp.concatenate(parts, axis=0)
    swap = [(0, 1), (1, 0)]
    tokens = jnp.concatenate([half, lax.ppermute(half, "core", swap)], axis=0)
    dq, own, other = attend_backward(qg, tokens)
    own = (own + lax.ppermute(other, "core", swap)).reshape(around, *kv.shape)
    total = own[0]
    for k in range(1, around):
        total = total + lax.ppermute(own[k].astype(low), "y", ring(-k, around)).astype(
            jnp.float32
        )
    out = jnp.concatenate([dq, total.astype(low).reshape(HEADS, 64, WIDE)], axis=1)
    return tuple(unpack(spread(out)))


def solution(mesh):
    fine = Mesh(
        mesh.devices.reshape(4, 2, 4, 2, 2), ("y", "xh", "z", "xl", "core")
    )
    queries = P(("y", "xh", "z", "xl", "core"), None)
    tokens = P(("z", "xl", "core", "y", "xh"), None)
    return jax.shard_map(
        functools.partial(per_device, around=4),
        mesh=fine,
        in_specs=(queries, tokens, tokens, queries),
        out_specs=(queries, tokens, tokens),
        check_vma=False,
    )
```

```python
import jax
import jax.numpy as jnp
from jax import lax
from jax.experimental import pallas as pl
from jax.experimental.pallas import tpu as pltpu
from jax.sharding import Mesh, PartitionSpec as P

HEADS = 16
HEAD_DIM = 64
WIDE = 2 * HEAD_DIM
LOG2E = 1.4426950408889634
NN = (((1,), (0,)), ((), ()))
CHIPS = ("y", "xh", "z", "xl")
RINGS = 4
BLOCK = 64
SHARE = BLOCK // RINGS
QUERY_BLOCK = 512
GROUP = 2048
PARAMS = pltpu.CompilerParams(
    vmem_limit_bytes=48 * 2**20, dimension_semantics=("arbitrary",)
)


def dot(left, right):
    return lax.dot_general(left, right, NN, preferred_element_type=jnp.float32)


def fold(values, op):
    return op(values.reshape(values.shape[0] // 8, 8, values.shape[1]), axis=0)


def over_rows(start, rows, step, unroll, body, carry):
    def iteration(i, carry):
        for j in range(unroll // step):
            carry = body(pl.multiple_of(start + i * unroll + j * step, step), carry)
        return carry

    return lax.fori_loop(0, rows // unroll, iteration, carry)


def head_kernel(
    mine_ref, pair_ref, dq_ref, own_ref, other_ref, e_ref, slope_ref, kt_ref, sum_ref, dqt_ref, stat_ref
):
    step = pl.program_id(0)
    sources = mine_ref.shape[0]
    half = sources * BLOCK
    tokens = 2 * half
    blocks = sources * SHARE // QUERY_BLOCK
    low = jnp.bfloat16

    def operands(block):
        each = QUERY_BLOCK // SHARE
        qg = mine_ref[block * each : (block + 1) * each, BLOCK:, :].reshape(QUERY_BLOCK, WIDE)
        lane = lax.broadcasted_iota(jnp.int32, qg.shape, 1)
        zero = jnp.zeros_like(qg)
        query = jnp.where(lane < HEAD_DIM, qg * low(HEAD_DIM**-0.5), zero)
        return query, jnp.where(lane < HEAD_DIM, zero, qg)

    def statistics(block, query, grad):
        query_t, grad_t = query.T, grad.T
        size = 512

        def tokens_at(ref, first):
            first = first // BLOCK
            return ref[pl.ds(first, size // BLOCK), :BLOCK, :].reshape(size, WIDE)

        def scores_of(ref, offset):
            def body(first, peak):
                kv = tokens_at(ref, first)
                rows = pl.ds(first + offset, size)
                scores = dot(kv, query_t) * LOG2E
                e_ref[rows, :] = scores
                if block == 0:
                    kt_ref[:, rows] = kv.T[:HEAD_DIM]
                return jnp.maximum(peak, fold(scores, jnp.max))

            return body

        peak = jnp.full((8, QUERY_BLOCK), -jnp.inf, jnp.float32)
        for ref, offset in ((mine_ref, 0), (pair_ref, half)):
            peak = over_rows(0, half, size, half, scores_of(ref, offset), peak)
        peak = jnp.max(peak, axis=0, keepdims=True)

        def sums_of(ref, offset):
            def body(first, carry):
                total, delta = carry
                rows = pl.ds(pl.multiple_of(first + offset, size), size)
                slopes = dot(tokens_at(ref, first), grad_t)
                slope_ref[rows, :] = slopes
                e = jnp.exp2(e_ref[rows, :] - peak)
                e_ref[rows, :] = e
                return total + fold(e, jnp.sum), delta + fold(e * slopes, jnp.sum)

            return body

        sums = (jnp.zeros((8, QUERY_BLOCK), jnp.float32),) * 2
        for ref, offset in ((mine_ref, 0), (pair_ref, half)):
            sums = over_rows(0, half, size, GROUP, sums_of(ref, offset), sums)
        total, delta = sums
        inverse = 1.0 / jnp.sum(total, axis=0, keepdims=True)
        return inverse, jnp.sum(delta, axis=0, keepdims=True) * inverse

    def gradients(first, rows, query, grad, inverse, delta, put, dq_t):
        both = jnp.concatenate([query, grad], axis=0)

        def part(first, dq_t):
            rows = pl.ds(first, 256)
            probs = e_ref[rows, :] * inverse
            weights = (probs * (slope_ref[rows, :] - delta)).astype(low)
            put(first, dot(jnp.concatenate([weights, probs.astype(low)], axis=1), both))
            return dq_t + dot(kt_ref[:, rows], weights)

        return over_rows(first, rows, 256, GROUP, part, dq_t)

    def put_dq(block, dq_t):
        dq = (dq_t.T * HEAD_DIM**-0.5).astype(low)
        dq = jnp.concatenate([dq, jnp.zeros_like(dq)], axis=1)
        each = QUERY_BLOCK // SHARE
        dq_ref[block * each : (block + 1) * each] = dq.reshape(each, SHARE, WIDE)

    @pl.when(step == 0)
    def _():
        for block in range(blocks):
            query, grad = operands(block)
            inverse, delta = statistics(block, query, grad)
            if block == blocks - 1:
                stat_ref[0:1, :] = inverse
                stat_ref[1:2, :] = delta
                break

            def put(first, part):
                rows = pl.ds(first, 256)
                sum_ref[rows, :] = part if block == 0 else sum_ref[rows, :] + part

            dq_t = gradients(
                0, tokens, query, grad, inverse, delta, put, jnp.zeros(dqt_ref.shape, jnp.float32)
            )
            put_dq(block, dq_t)
        dqt_ref[...] = jnp.zeros_like(dqt_ref)

    query, grad = operands(blocks - 1)

    def last(first, out_ref):
        def put(row, part):
            rows = pl.ds(pl.multiple_of(row - first, 256), 256)
            out_ref[rows, :] = (sum_ref[pl.ds(row, 256), :] + part).astype(out_ref.dtype)

        dqt_ref[...] = gradients(
            first, GROUP, query, grad, stat_ref[0:1, :], stat_ref[1:2, :], put, dqt_ref[...]
        )

    per_half = half // GROUP

    @pl.when(step < per_half)
    def _():
        last(half + step * GROUP, other_ref)

    @pl.when(step >= per_half)
    def _():
        last((step - per_half) * GROUP, own_ref)

    @pl.when(step == 2 * per_half - 1)
    def _():
        put_dq(blocks - 1, dqt_ref[...])


def attend_backward(mine, pair):
    sources = mine.shape[0]
    half = sources * BLOCK
    per_half = half // GROUP
    return pl.pallas_call(
        head_kernel,
        grid=(2 * per_half,),
        in_specs=[pl.BlockSpec(mine.shape, lambda i: (0, 0, 0))] * 2,
        out_specs=[
            pl.BlockSpec((sources, SHARE, WIDE), lambda i: (0, 0, 0)),
            pl.BlockSpec((GROUP, WIDE), lambda i: (jnp.maximum(i - per_half, 0), 0)),
            pl.BlockSpec((GROUP, WIDE), lambda i: (jnp.minimum(i, per_half - 1), 0)),
        ],
        out_shape=[
            jax.ShapeDtypeStruct((sources, SHARE, WIDE), jnp.bfloat16),
            jax.ShapeDtypeStruct((half, WIDE), jnp.float32),
            jax.ShapeDtypeStruct((half, WIDE), jnp.bfloat16),
        ],
        scratch_shapes=[
            pltpu.VMEM((2 * half, QUERY_BLOCK), jnp.float32),
            pltpu.VMEM((2 * half, QUERY_BLOCK), jnp.float32),
            pltpu.VMEM((HEAD_DIM, 2 * half), jnp.bfloat16),
            pltpu.VMEM((2 * half, WIDE), jnp.float32),
            pltpu.VMEM((HEAD_DIM, QUERY_BLOCK), jnp.float32),
            pltpu.VMEM((8, QUERY_BLOCK), jnp.float32),
        ],
        compiler_params=PARAMS,
    )(mine, pair)


def whole():
    return pl.BlockSpec(memory_space=pltpu.VMEM)


def pack_kernel(q_ref, k_ref, v_ref, g_ref, out_ref):
    for head in range(HEADS):
        columns = slice(head * HEAD_DIM, (head + 1) * HEAD_DIM)
        kv = jnp.concatenate([k_ref[:, columns], v_ref[:, columns]], axis=1)
        qg = jnp.concatenate([q_ref[:, columns], g_ref[:, columns]], axis=1)
        for ring in range(RINGS):
            out_ref[ring * HEADS + head, :BLOCK] = kv
            out_ref[ring * HEADS + head, BLOCK:] = qg[ring * SHARE : (ring + 1) * SHARE]


def pack(query, key, value, grad):
    return pl.pallas_call(
        pack_kernel,
        in_specs=[whole()] * 4,
        out_specs=whole(),
        out_shape=pltpu.VMEM((RINGS * HEADS, BLOCK + SHARE, WIDE), query.dtype),
    )(query, key, value, grad)


def unpack_kernel(in_ref, dq_ref, dk_ref, dv_ref):
    for pair in range(HEADS // 2):
        columns = slice(pair * WIDE, (pair + 1) * WIDE)
        sums = [0.0, 0.0]
        for ring in range(RINGS):
            one, two = (
                in_ref[ring * HEADS + 2 * pair + i].astype(jnp.float32) for i in range(2)
            )
            sums = [sums[0] + one[:BLOCK], sums[1] + two[:BLOCK]]
            dq_ref[ring * SHARE : (ring + 1) * SHARE, columns] = jnp.concatenate(
                [one[BLOCK:, :HEAD_DIM], two[BLOCK:, :HEAD_DIM]], axis=1
            )
        one, two = sums
        dk_ref[:, columns] = jnp.concatenate([one[:, :HEAD_DIM], two[:, :HEAD_DIM]], axis=1)
        dv_ref[:, columns] = jnp.concatenate([one[:, HEAD_DIM:], two[:, HEAD_DIM:]], axis=1)


def unpack(parts):
    out = jax.ShapeDtypeStruct((BLOCK, HEADS * HEAD_DIM), jnp.float32)
    return pl.pallas_call(
        unpack_kernel, in_specs=[whole()], out_specs=[whole()] * 3, out_shape=[out] * 3
    )(parts)


def combine_kernel(own_ref, other_ref, dq_ref, out_ref):
    total = own_ref[...] + other_ref[...].astype(jnp.float32)
    out_ref[:, :BLOCK] = total.astype(out_ref.dtype).reshape(-1, BLOCK, WIDE)
    out_ref[:, BLOCK:] = dq_ref[...]


def combine(own, other, dq):
    return pl.pallas_call(
        combine_kernel,
        in_specs=[whole()] * 3,
        out_specs=whole(),
        out_shape=pltpu.VMEM((dq.shape[0], BLOCK + SHARE, WIDE), dq.dtype),
    )(own, other, dq)


def per_device(query_proj, key_proj, value_proj, grad_attn):
    def spread(packed):
        return lax.all_to_all(packed, CHIPS, 0, 0, tiled=True)

    def swap(values):
        return lax.ppermute(values, "core", [(0, 1), (1, 0)])

    mine = spread(pack(query_proj, key_proj, value_proj, grad_attn))
    dq, own, other = attend_backward(mine, swap(mine))
    return tuple(unpack(spread(combine(own, swap(other), dq))))


def solution(mesh):
    fine = Mesh(
        mesh.devices.reshape(RINGS, 2, 4, 2, 2), ("y", "xh", "z", "xl", "core")
    )
    queries = P(("y", "xh", "z", "xl", "core"), None)
    tokens = P(("z", "xl", "core", "y", "xh"), None)
    return jax.shard_map(
        per_device,
        mesh=fine,
        in_specs=(queries, tokens, tokens, queries),
        out_specs=(queries, tokens, tokens),
        check_vma=False,
    )
```

```python
import jax
import jax.numpy as jnp
from jax import lax
from jax.experimental import pallas as pl
from jax.experimental.pallas import tpu as pltpu
from jax.sharding import Mesh, PartitionSpec as P

HEADS = 16
HEAD_DIM = 64
WIDE = 2 * HEAD_DIM
LOG2E = 1.4426950408889634
NN = (((1,), (0,)), ((), ()))
CHIPS = ("y", "xh", "z", "xl")
RINGS = 4
BLOCK = 64
SHARE = BLOCK // RINGS
QUERY_BLOCK = 512
GROUP = 2048
STEP = 512


def dot(left, right):
    return lax.dot_general(left, right, NN, preferred_element_type=jnp.float32)


def fold(values, op):
    return op(values.reshape(values.shape[0] // 8, 8, values.shape[1]), axis=0)


def over_rows(start, rows, step, unroll, body, carry):
    def iteration(i, carry):
        for j in range(unroll // step):
            carry = body(pl.multiple_of(start + i * unroll + j * step, step), carry)
        return carry

    return lax.fori_loop(0, rows // unroll, iteration, carry)


def operands(mine_ref, block):
    each = QUERY_BLOCK // SHARE
    qg = mine_ref[block * each : (block + 1) * each, BLOCK:, :].reshape(QUERY_BLOCK, WIDE)
    lane = lax.broadcasted_iota(jnp.int32, qg.shape, 1)
    zero = jnp.zeros_like(qg)
    query = jnp.where(lane < HEAD_DIM, qg * jnp.bfloat16(HEAD_DIM**-0.5), zero)
    return query, jnp.where(lane < HEAD_DIM, zero, qg)


def tokens_at(ref, first):
    return ref[pl.ds(first // BLOCK, STEP // BLOCK), :BLOCK, :].reshape(STEP, WIDE)


def add_scores(half, query_t, peak, grad_t=None, keep_turned=False):
    kv_ref, e_ref, slope_ref, kt_ref = half

    def body(first, peak):
        kv = tokens_at(kv_ref, first)
        rows = pl.ds(first, STEP)
        scores = dot(kv, query_t) * LOG2E
        e_ref[rows, :] = scores
        if grad_t is not None:
            slope_ref[rows, :] = dot(kv, grad_t)
        if keep_turned:
            kt_ref[:, rows] = kv.T[:HEAD_DIM]
        return jnp.maximum(peak, fold(scores, jnp.max))

    rows = e_ref.shape[0]
    return over_rows(0, rows, STEP, rows, body, peak)


def add_sums(half, grad_t, peak, sums):
    kv_ref, e_ref, slope_ref, _ = half

    def body(first, carry):
        total, delta = carry
        rows = pl.ds(first, STEP)
        if grad_t is None:
            slopes = slope_ref[rows, :]
        else:
            slopes = dot(tokens_at(kv_ref, first), grad_t)
            slope_ref[rows, :] = slopes
        e = jnp.exp2(e_ref[rows, :] - peak)
        e_ref[rows, :] = e
        return total + fold(e, jnp.sum), delta + fold(e * slopes, jnp.sum)

    return over_rows(0, e_ref.shape[0], STEP, GROUP, body, sums)


def add_gradients(half, query, grad, inverse, delta, put, dq_t):
    _, e_ref, slope_ref, kt_ref = half
    both = jnp.concatenate([query, grad], axis=0)

    def body(first, dq_t):
        rows = pl.ds(first, 256)
        probs = e_ref[rows, :] * inverse
        weights = (probs * (slope_ref[rows, :] - delta)).astype(jnp.bfloat16)
        pair = jnp.concatenate([weights, probs.astype(jnp.bfloat16)], axis=1)
        put(rows, dot(pair, both))
        return dq_t + dot(kt_ref[:, rows], weights)

    return over_rows(0, e_ref.shape[0], 256, GROUP, body, dq_t)


def dq_rows(dq_t):
    dq = (dq_t * HEAD_DIM**-0.5).T.astype(jnp.bfloat16)
    dq = jnp.concatenate([dq, jnp.zeros_like(dq)], axis=1)
    return dq.reshape(QUERY_BLOCK // SHARE, SHARE, WIDE)


def start_kernel(mine_ref, e_ref, slope_ref, kt_ref, peak_ref):
    query, grad = operands(mine_ref, 0)
    peak = jnp.full(peak_ref.shape, -jnp.inf, jnp.float32)
    half = (mine_ref, e_ref, slope_ref, kt_ref)
    peak_ref[...] = add_scores(half, query.T, peak, grad.T, keep_turned=True)


def main_kernel(
    mine_ref, pair_ref, e_in, slope_in, kt_ref, peak_ref,
    e_ref, slope_ref, other_ref, own_ref, dq_ref, dqt_ref, stat_ref,
    e_pair, slope_pair, kt_pair, sum_pair,
):
    del e_in, slope_in
    mine = (mine_ref, e_ref, slope_ref, kt_ref)
    pair = (pair_ref, e_pair, slope_pair, kt_pair)
    none = jnp.zeros((8, QUERY_BLOCK), jnp.float32)

    def ratios(sums):
        total, delta = (jnp.sum(x, axis=0, keepdims=True) for x in sums)
        inverse = 1.0 / total
        return inverse, delta * inverse

    query, grad = operands(mine_ref, 0)
    grad_t = grad.T
    peak = add_scores(pair, query.T, peak_ref[...], keep_turned=True)
    peak = jnp.max(peak, axis=0, keepdims=True)
    sums = add_sums(mine, None, peak, (none, none))
    inverse, delta = ratios(add_sums(pair, grad_t, peak, sums))

    def put_own(rows, part):
        own_ref[rows, :] = part

    def put_pair(rows, part):
        sum_pair[rows, :] = part

    dq_t = jnp.zeros(dqt_ref.shape, jnp.float32)
    dq_t = add_gradients(mine, query, grad, inverse, delta, put_own, dq_t)
    dq_t = add_gradients(pair, query, grad, inverse, delta, put_pair, dq_t)
    dq_ref[...] = dq_rows(dq_t)

    query, grad = operands(mine_ref, 1)
    query_t, grad_t = query.T, grad.T
    peak = add_scores(mine, query_t, jnp.full_like(none, -jnp.inf))
    peak = jnp.max(add_scores(pair, query_t, peak), axis=0, keepdims=True)
    sums = add_sums(mine, grad_t, peak, (none, none))
    inverse, delta = ratios(add_sums(pair, grad_t, peak, sums))

    def put_other(rows, part):
        other_ref[rows, :] = (sum_pair[rows, :] + part).astype(other_ref.dtype)

    dqt_ref[...] = add_gradients(
        pair, query, grad, inverse, delta, put_other, jnp.zeros(dqt_ref.shape, jnp.float32)
    )
    stat_ref[0:1, :] = inverse
    stat_ref[1:2, :] = delta


def end_kernel(
    mine_ref, e_ref, slope_ref, kt_ref, own_in, dqt_ref, stat_ref, own_ref, dq_ref
):
    def put(rows, part):
        own_ref[rows, :] = own_in[rows, :] + part

    query, grad = operands(mine_ref, 1)
    dq_t = add_gradients(
        (mine_ref, e_ref, slope_ref, kt_ref),
        query, grad, stat_ref[0:1, :], stat_ref[1:2, :], put, dqt_ref[...],
    )
    dq_ref[...] = dq_rows(dq_t)


def call(kernel, arrays, outs, scratch=(), limit=8, aliases=None):
    return pl.pallas_call(
        kernel,
        in_specs=[pl.BlockSpec(memory_space=pltpu.VMEM)] * len(arrays),
        out_specs=[pl.BlockSpec(memory_space=pltpu.VMEM)] * len(outs),
        out_shape=[out if hasattr(out, "dtype") else pltpu.VMEM(*out) for out in outs],
        scratch_shapes=[pltpu.VMEM(*shape) for shape in scratch],
        input_output_aliases=aliases or {},
        compiler_params=pltpu.CompilerParams(vmem_limit_bytes=limit * 2**20),
    )(*(pltpu.with_memory_space_constraint(x, pltpu.VMEM) for x in arrays))


def pack_kernel(q_ref, k_ref, v_ref, g_ref, out_ref):
    for head in range(HEADS):
        columns = slice(head * HEAD_DIM, (head + 1) * HEAD_DIM)
        kv = jnp.concatenate([k_ref[:, columns], v_ref[:, columns]], axis=1)
        qg = jnp.concatenate([q_ref[:, columns], g_ref[:, columns]], axis=1)
        for ring in range(RINGS):
            out_ref[ring * HEADS + head, :BLOCK] = kv
            out_ref[ring * HEADS + head, BLOCK:] = qg[ring * SHARE : (ring + 1) * SHARE]


def pack(query, key, value, grad):
    shape = (RINGS * HEADS, BLOCK + SHARE, WIDE)
    return call(pack_kernel, (query, key, value, grad), [(shape, query.dtype)])[0]


def unpack_kernel(in_ref, dq_ref, dk_ref, dv_ref):
    for pair in range(HEADS // 2):
        columns = slice(pair * WIDE, (pair + 1) * WIDE)
        sums = [0.0, 0.0]
        for ring in range(RINGS):
            one, two = (
                in_ref[ring * HEADS + 2 * pair + i].astype(jnp.float32) for i in range(2)
            )
            sums = [sums[0] + one[:BLOCK], sums[1] + two[:BLOCK]]
            dq_ref[ring * SHARE : (ring + 1) * SHARE, columns] = jnp.concatenate(
                [one[BLOCK:, :HEAD_DIM], two[BLOCK:, :HEAD_DIM]], axis=1
            )
        one, two = sums
        dk_ref[:, columns] = jnp.concatenate([one[:, :HEAD_DIM], two[:, :HEAD_DIM]], axis=1)
        dv_ref[:, columns] = jnp.concatenate([one[:, HEAD_DIM:], two[:, HEAD_DIM:]], axis=1)


def unpack(parts):
    out = jax.ShapeDtypeStruct((BLOCK, HEADS * HEAD_DIM), jnp.float32)
    return call(unpack_kernel, (parts,), [out] * 3)


def combine_kernel(own_ref, other_ref, dq0_ref, dq1_ref, out_ref):
    total = own_ref[...] + other_ref[...].astype(jnp.float32)
    out_ref[:, :BLOCK] = total.astype(out_ref.dtype).reshape(-1, BLOCK, WIDE)
    each = dq0_ref.shape[0]
    out_ref[:each, BLOCK:] = dq0_ref[...]
    out_ref[each:, BLOCK:] = dq1_ref[...]


def per_device(query_proj, key_proj, value_proj, grad_attn):
    low, full = jnp.bfloat16, jnp.float32

    def spread(packed):
        return lax.all_to_all(packed, CHIPS, 0, 0, tiled=True)

    def swap(values):
        return lax.ppermute(values, "core", [(0, 1), (1, 0)])

    mine = spread(pack(query_proj, key_proj, value_proj, grad_attn))
    half = mine.shape[0] * BLOCK
    wide = ((half, QUERY_BLOCK), full)
    turned = ((HEAD_DIM, half), low)
    total = ((half, WIDE), full)
    dq_shape = ((QUERY_BLOCK // SHARE, SHARE, WIDE), low)
    dqt = ((HEAD_DIM, QUERY_BLOCK), full)
    eight = ((8, QUERY_BLOCK), full)
    pair = swap(mine)
    e, slope, kt, peak = call(start_kernel, (mine,), [wide, wide, turned, eight])
    e, slope, other, own, dq0, dq_t, stats = call(
        main_kernel,
        (mine, pair, e, slope, kt, peak),
        [wide, wide, ((half, WIDE), low), total, dq_shape, dqt, eight],
        scratch=[wide, wide, turned, total],
        limit=22,
        aliases={2: 0, 3: 1},
    )
    other = swap(other)
    own, dq1 = call(
        end_kernel, (mine, e, slope, kt, own, dq_t, stats), [total, dq_shape], aliases={4: 0}
    )
    back = call(combine_kernel, (own, other, dq0, dq1), [(mine.shape, low)])[0]
    return tuple(unpack(spread(back)))


def solution(mesh):
    fine = Mesh(
        mesh.devices.reshape(RINGS, 2, 4, 2, 2), ("y", "xh", "z", "xl", "core")
    )
    queries = P(("y", "xh", "z", "xl", "core"), None)
    tokens = P(("z", "xl", "core", "y", "xh"), None)
    return jax.shard_map(
        per_device,
        mesh=fine,
        in_specs=(queries, tokens, tokens, queries),
        out_specs=(queries, tokens, tokens),
        check_vma=False,
    )
```

```python
import jax
import jax.numpy as jnp
from jax import lax
from jax.experimental import pallas as pl
from jax.experimental.pallas import tpu as pltpu
from jax.sharding import Mesh, PartitionSpec as P

HEADS = 16
HEAD_DIM = 64
WIDE = 2 * HEAD_DIM
LOG2E = 1.4426950408889634
NN = (((1,), (0,)), ((), ()))
CHIPS = ("xl", "xh", "z", "y")
RINGS = 4
BLOCK = 64
SHARE = BLOCK // RINGS
QUERY_BLOCK = 512
GROUP = 2048
STEP = 512


def dot(left, right):
    return lax.dot_general(left, right, NN, preferred_element_type=jnp.float32)


def fold(values, op):
    return op(values.reshape(values.shape[0] // 8, 8, values.shape[1]), axis=0)


def over_rows(start, rows, step, unroll, body, carry):
    def iteration(i, carry):
        for j in range(unroll // step):
            carry = body(pl.multiple_of(start + i * unroll + j * step, step), carry)
        return carry

    return lax.fori_loop(0, rows // unroll, iteration, carry)


def operands(mine_ref, block):
    each = QUERY_BLOCK // SHARE
    qg = mine_ref[block * each : (block + 1) * each, BLOCK:, :].reshape(QUERY_BLOCK, WIDE)
    lane = lax.broadcasted_iota(jnp.int32, qg.shape, 1)
    zero = jnp.zeros_like(qg)
    query = jnp.where(lane < HEAD_DIM, qg * jnp.bfloat16(HEAD_DIM**-0.5), zero)
    return query, jnp.where(lane < HEAD_DIM, zero, qg)


def tokens_at(ref, first):
    return ref[pl.ds(first // BLOCK, STEP // BLOCK), :BLOCK, :].reshape(STEP, WIDE)


def add_scores(half, query_t, peak, grad_t=None, keep_turned=False):
    kv_ref, e_ref, slope_ref, kt_ref = half

    def body(first, peak):
        kv = tokens_at(kv_ref, first)
        rows = pl.ds(first, STEP)
        scores = dot(kv, query_t) * LOG2E
        e_ref[rows, :] = scores
        if grad_t is not None:
            slope_ref[rows, :] = dot(kv, grad_t)
        if keep_turned:
            kt_ref[:, rows] = kv.T[:HEAD_DIM]
        return jnp.maximum(peak, fold(scores, jnp.max))

    rows = e_ref.shape[0]
    return over_rows(0, rows, STEP, rows, body, peak)


def add_sums(half, grad_t, peak, sums):
    kv_ref, e_ref, slope_ref, _ = half

    def body(first, carry):
        total, delta = carry
        rows = pl.ds(first, STEP)
        if grad_t is None:
            slopes = slope_ref[rows, :]
        else:
            slopes = dot(tokens_at(kv_ref, first), grad_t)
            slope_ref[rows, :] = slopes
        e = jnp.exp2(e_ref[rows, :] - peak)
        e_ref[rows, :] = e
        return total + fold(e, jnp.sum), delta + fold(e * slopes, jnp.sum)

    return over_rows(0, e_ref.shape[0], STEP, GROUP, body, sums)


def add_gradients(half, query, grad, inverse, delta, put, dq_t):
    _, e_ref, slope_ref, kt_ref = half
    both = jnp.concatenate([query, grad], axis=0)

    def body(first, dq_t):
        rows = pl.ds(first, 256)
        probs = e_ref[rows, :] * inverse
        weights = (probs * (slope_ref[rows, :] - delta)).astype(jnp.bfloat16)
        pair = jnp.concatenate([weights, probs.astype(jnp.bfloat16)], axis=1)
        put(rows, dot(pair, both))
        return dq_t + dot(kt_ref[:, rows], weights)

    return over_rows(0, e_ref.shape[0], 256, GROUP, body, dq_t)


def dq_rows(dq_t):
    dq = (dq_t * HEAD_DIM**-0.5).T.astype(jnp.bfloat16)
    dq = jnp.concatenate([dq, jnp.zeros_like(dq)], axis=1)
    return dq.reshape(QUERY_BLOCK // SHARE, SHARE, WIDE)


def start_kernel(mine_ref, e_ref, slope_ref, kt_ref, peak_ref):
    query, grad = operands(mine_ref, 0)
    peak = jnp.full(peak_ref.shape, -jnp.inf, jnp.float32)
    half = (mine_ref, e_ref, slope_ref, kt_ref)
    peak_ref[...] = add_scores(half, query.T, peak, grad.T, keep_turned=True)


def main_kernel(
    mine_ref, pair_ref, e_in, slope_in, kt_ref, peak_ref,
    e_ref, slope_ref, other_ref, own_ref, dq_ref, dqt_ref, stat_ref,
    e_pair, slope_pair, kt_pair, sum_pair,
):
    del e_in, slope_in
    mine = (mine_ref, e_ref, slope_ref, kt_ref)
    pair = (pair_ref, e_pair, slope_pair, kt_pair)
    none = jnp.zeros((8, QUERY_BLOCK), jnp.float32)

    def ratios(sums):
        total, delta = (jnp.sum(x, axis=0, keepdims=True) for x in sums)
        inverse = 1.0 / total
        return inverse, delta * inverse

    query, grad = operands(mine_ref, 0)
    grad_t = grad.T
    peak = add_scores(pair, query.T, peak_ref[...], keep_turned=True)
    peak = jnp.max(peak, axis=0, keepdims=True)
    sums = add_sums(mine, None, peak, (none, none))
    inverse, delta = ratios(add_sums(pair, grad_t, peak, sums))

    def put_own(rows, part):
        own_ref[rows, :] = part

    def put_pair(rows, part):
        sum_pair[rows, :] = part

    dq_t = jnp.zeros(dqt_ref.shape, jnp.float32)
    dq_t = add_gradients(mine, query, grad, inverse, delta, put_own, dq_t)
    dq_t = add_gradients(pair, query, grad, inverse, delta, put_pair, dq_t)
    dq_ref[...] = dq_rows(dq_t)

    query, grad = operands(mine_ref, 1)
    query_t, grad_t = query.T, grad.T
    peak = add_scores(mine, query_t, jnp.full_like(none, -jnp.inf))
    peak = jnp.max(add_scores(pair, query_t, peak), axis=0, keepdims=True)
    sums = add_sums(mine, grad_t, peak, (none, none))
    inverse, delta = ratios(add_sums(pair, grad_t, peak, sums))

    def put_other(rows, part):
        other_ref[rows, :] = (sum_pair[rows, :] + part).astype(other_ref.dtype)

    dqt_ref[...] = add_gradients(
        pair, query, grad, inverse, delta, put_other, jnp.zeros(dqt_ref.shape, jnp.float32)
    )
    stat_ref[0:1, :] = inverse
    stat_ref[1:2, :] = delta


def end_kernel(
    mine_ref, e_ref, slope_ref, kt_ref, own_in, dqt_ref, stat_ref, own_ref, dq_ref
):
    def put(rows, part):
        own_ref[rows, :] = own_in[rows, :] + part

    query, grad = operands(mine_ref, 1)
    dq_t = add_gradients(
        (mine_ref, e_ref, slope_ref, kt_ref),
        query, grad, stat_ref[0:1, :], stat_ref[1:2, :], put, dqt_ref[...],
    )
    dq_ref[...] = dq_rows(dq_t)


def call(kernel, arrays, outs, scratch=(), limit=8, aliases=None, stay=True):
    return pl.pallas_call(
        kernel,
        in_specs=[pl.BlockSpec(memory_space=pltpu.VMEM)] * len(arrays),
        out_specs=[pl.BlockSpec(memory_space=pltpu.VMEM)] * len(outs),
        out_shape=[out if hasattr(out, "dtype") else pltpu.VMEM(*out) for out in outs],
        scratch_shapes=[pltpu.VMEM(*shape) for shape in scratch],
        input_output_aliases=aliases or {},
        compiler_params=pltpu.CompilerParams(vmem_limit_bytes=limit * 2**20),
    )(*(pltpu.with_memory_space_constraint(x, pltpu.VMEM) if stay else x for x in arrays))


def pack_kernel(q_ref, k_ref, v_ref, g_ref, out_ref):
    for head in range(HEADS):
        columns = slice(head * HEAD_DIM, (head + 1) * HEAD_DIM)
        kv = jnp.concatenate([k_ref[:, columns], v_ref[:, columns]], axis=1)
        qg = jnp.concatenate([q_ref[:, columns], g_ref[:, columns]], axis=1)
        for ring in range(RINGS):
            out_ref[head * RINGS + ring, :BLOCK] = kv
            out_ref[head * RINGS + ring, BLOCK:] = qg[ring * SHARE : (ring + 1) * SHARE]


def pack(query, key, value, grad):
    shape = (RINGS * HEADS, BLOCK + SHARE, WIDE)
    return call(pack_kernel, (query, key, value, grad), [(shape, query.dtype)], stay=False)[0]


def unpack_kernel(in_ref, dq_ref, dk_ref, dv_ref):
    for pair in range(HEADS // 2):
        columns = slice(pair * WIDE, (pair + 1) * WIDE)
        sums = [0.0, 0.0]
        for ring in range(RINGS):
            one, two = (
                in_ref[(2 * pair + i) * RINGS + ring].astype(jnp.float32) for i in range(2)
            )
            sums = [sums[0] + one[:BLOCK], sums[1] + two[:BLOCK]]
            dq_ref[ring * SHARE : (ring + 1) * SHARE, columns] = jnp.concatenate(
                [one[BLOCK:, :HEAD_DIM], two[BLOCK:, :HEAD_DIM]], axis=1
            )
        one, two = sums
        dk_ref[:, columns] = jnp.concatenate([one[:, :HEAD_DIM], two[:, :HEAD_DIM]], axis=1)
        dv_ref[:, columns] = jnp.concatenate([one[:, HEAD_DIM:], two[:, HEAD_DIM:]], axis=1)


def unpack(parts):
    out = jax.ShapeDtypeStruct((BLOCK, HEADS * HEAD_DIM), jnp.float32)
    return call(unpack_kernel, (parts,), [out] * 3)


def combine_kernel(own_ref, other_ref, dq0_ref, dq1_ref, out_ref):
    total = own_ref[...] + other_ref[...].astype(jnp.float32)
    out_ref[:, :BLOCK] = total.astype(out_ref.dtype).reshape(-1, BLOCK, WIDE)
    each = dq0_ref.shape[0]
    out_ref[:each, BLOCK:] = dq0_ref[...]
    out_ref[each:, BLOCK:] = dq1_ref[...]


def per_device(query_proj, key_proj, value_proj, grad_attn):
    low, full = jnp.bfloat16, jnp.float32

    def spread(packed):
        return lax.all_to_all(packed, CHIPS, 0, 0, tiled=True)

    def swap(values):
        return lax.ppermute(values, "core", [(0, 1), (1, 0)])

    mine = spread(pack(query_proj, key_proj, value_proj, grad_attn))
    half = mine.shape[0] * BLOCK
    wide = ((half, QUERY_BLOCK), full)
    turned = ((HEAD_DIM, half), low)
    total = ((half, WIDE), full)
    dq_shape = ((QUERY_BLOCK // SHARE, SHARE, WIDE), low)
    dqt = ((HEAD_DIM, QUERY_BLOCK), full)
    eight = ((8, QUERY_BLOCK), full)
    pair = swap(mine)
    e, slope, kt, peak = call(start_kernel, (mine,), [wide, wide, turned, eight])
    e, slope, other, own, dq0, dq_t, stats = call(
        main_kernel,
        (mine, pair, e, slope, kt, peak),
        [wide, wide, ((half, WIDE), low), total, dq_shape, dqt, eight],
        scratch=[wide, wide, turned, total],
        limit=22,
        aliases={2: 0, 3: 1},
    )
    other = swap(other)
    own, dq1 = call(
        end_kernel, (mine, e, slope, kt, own, dq_t, stats), [total, dq_shape], aliases={4: 0}
    )
    back = call(combine_kernel, (own, other, dq0, dq1), [(mine.shape, low)])[0]
    return tuple(unpack(spread(back)))


def solution(mesh):
    fine = Mesh(
        mesh.devices.reshape(RINGS, 2, 4, 2, 2), ("y", "xh", "z", "xl", "core")
    )
    queries = P(("y", "xh", "z", "xl", "core"), None)
    tokens = P(("z", "xl", "core", "y", "xh"), None)
    return jax.shard_map(
        per_device,
        mesh=fine,
        in_specs=(queries, tokens, tokens, queries),
        out_specs=(queries, tokens, tokens),
        check_vma=False,
    )
```

```python
import jax
import jax.numpy as jnp
from jax import lax
from jax.experimental import pallas as pl
from jax.experimental.pallas import tpu as pltpu
from jax.sharding import Mesh, PartitionSpec as P

HEADS = 16
HEAD_DIM = 64
WIDE = 2 * HEAD_DIM
LOG2E = 1.4426950408889634
NN = (((1,), (0,)), ((), ()))
CHIPS = ("xl", "xh", "z", "y")
RINGS = 4
BLOCK = 64
SHARE = BLOCK // RINGS
QUERY_BLOCK = 512
GROUP = 2048
STEP = 512


def dot(left, right):
    return lax.dot_general(left, right, NN, preferred_element_type=jnp.float32)


def fold(values, op):
    return op(values.reshape(values.shape[0] // 8, 8, values.shape[1]), axis=0)


def over_rows(start, rows, step, unroll, body, carry):
    def iteration(i, carry):
        for j in range(unroll // step):
            carry = body(pl.multiple_of(start + i * unroll + j * step, step), carry)
        return carry

    return lax.fori_loop(0, rows // unroll, iteration, carry)


def operands(mine_ref, block):
    each = QUERY_BLOCK // SHARE
    qg = mine_ref[block * each : (block + 1) * each, BLOCK:, :].reshape(QUERY_BLOCK, WIDE)
    lane = lax.broadcasted_iota(jnp.int32, qg.shape, 1)
    zero = jnp.zeros_like(qg)
    query = jnp.where(lane < HEAD_DIM, qg * jnp.bfloat16(HEAD_DIM**-0.5), zero)
    return query, jnp.where(lane < HEAD_DIM, zero, qg)


def tokens_at(ref, first):
    return ref[pl.ds(first // BLOCK, STEP // BLOCK), :BLOCK, :].reshape(STEP, WIDE)


def add_scores(half, query_t, peak, keep_turned):
    kv_ref, e_ref, _, kt_ref = half

    def body(first, peak):
        kv = tokens_at(kv_ref, first)
        rows = pl.ds(first, STEP)
        scores = dot(kv, query_t) * LOG2E
        e_ref[rows, :] = scores
        if keep_turned:
            kt_ref[:, rows] = kv.T[:HEAD_DIM]
        return jnp.maximum(peak, fold(scores, jnp.max))

    rows = e_ref.shape[0]
    return over_rows(0, rows, STEP, rows, body, peak)


def add_sums(half, grad_t, peak, sums):
    kv_ref, e_ref, slope_ref, _ = half

    def body(first, carry):
        total, delta = carry
        rows = pl.ds(first, STEP)
        slopes = dot(tokens_at(kv_ref, first), grad_t)
        slope_ref[rows, :] = slopes
        e = jnp.exp2(e_ref[rows, :] - peak)
        e_ref[rows, :] = e
        return total + fold(e, jnp.sum), delta + fold(e * slopes, jnp.sum)

    return over_rows(0, e_ref.shape[0], STEP, GROUP, body, sums)


def add_gradients(half, query, grad, factor, delta, put, dq_t):
    _, e_ref, slope_ref, kt_ref = half
    both = jnp.concatenate([query, grad], axis=0)

    def body(first, dq_t):
        rows = pl.ds(first, 256)
        probs = e_ref[rows, :] * factor
        weights = (probs * (slope_ref[rows, :] - delta)).astype(jnp.bfloat16)
        pair = jnp.concatenate([weights, probs.astype(jnp.bfloat16)], axis=1)
        put(rows, dot(pair, both))
        return dq_t + dot(kt_ref[:, rows], weights)

    return over_rows(0, e_ref.shape[0], 256, GROUP, body, dq_t)


def dq_rows(dq_t):
    dq = (dq_t * HEAD_DIM**-0.5).T.astype(jnp.bfloat16)
    dq = jnp.concatenate([dq, jnp.zeros_like(dq)], axis=1)
    return dq.reshape(QUERY_BLOCK // SHARE, SHARE, WIDE)


NONE = float("-inf")


def half_sums(half, query_t, grad_t, keep_turned=False):
    count = query_t.shape[1]
    none = jnp.zeros((8, count), jnp.float32)
    peak = add_scores(half, query_t, jnp.full((8, count), NONE), keep_turned)
    peak = jnp.max(peak, axis=0, keepdims=True)
    sums = add_sums(half, grad_t, peak, (none, none))
    return (peak, *(jnp.sum(x, axis=0, keepdims=True) for x in sums))


def joined(one, two):
    peak = jnp.maximum(one[0], two[0])
    first, second = jnp.exp2(one[0] - peak), jnp.exp2(two[0] - peak)
    inverse = 1.0 / (one[1] * first + two[1] * second)
    delta = (one[2] * first + two[2] * second) * inverse
    return first * inverse, second * inverse, delta


def start_kernel(mine_ref, e_ref, slope_ref, kt_ref, stat_ref):
    query, grad = operands(mine_ref, 0)
    half = (mine_ref, e_ref, slope_ref, kt_ref)
    for i, row in enumerate(half_sums(half, query.T, grad.T, keep_turned=True)):
        stat_ref[i : i + 1, :] = row


def main_kernel(
    mine_ref, pair_ref, e_in, slope_in, kt_ref, first_ref,
    e_ref, slope_ref, other_ref, own_ref, dq_ref, dqt_ref, stat_ref,
    e_pair, slope_pair, kt_pair, sum_pair,
):
    del e_in, slope_in
    mine = (mine_ref, e_ref, slope_ref, kt_ref)
    pair = (pair_ref, e_pair, slope_pair, kt_pair)

    query, grad = operands(mine_ref, 0)
    own_sums = tuple(first_ref[i : i + 1, :] for i in range(3))
    pair_sums = half_sums(pair, query.T, grad.T, keep_turned=True)
    own_factor, pair_factor, delta = joined(own_sums, pair_sums)

    def put_own(rows, part):
        own_ref[rows, :] = part

    def put_pair(rows, part):
        sum_pair[rows, :] = part

    dq_t = jnp.zeros(dqt_ref.shape, jnp.float32)
    dq_t = add_gradients(mine, query, grad, own_factor, delta, put_own, dq_t)
    dq_t = add_gradients(pair, query, grad, pair_factor, delta, put_pair, dq_t)
    dq_ref[...] = dq_rows(dq_t)

    query, grad = operands(mine_ref, 1)
    query_t, grad_t = query.T, grad.T
    own_sums = half_sums(mine, query_t, grad_t)
    pair_sums = half_sums(pair, query_t, grad_t)
    own_factor, pair_factor, delta = joined(own_sums, pair_sums)

    def put_other(rows, part):
        other_ref[rows, :] = (sum_pair[rows, :] + part).astype(other_ref.dtype)

    dqt_ref[...] = add_gradients(
        pair, query, grad, pair_factor, delta, put_other, jnp.zeros(dqt_ref.shape, jnp.float32)
    )
    stat_ref[0:1, :] = own_factor
    stat_ref[1:2, :] = delta


def end_kernel(
    mine_ref, e_ref, slope_ref, kt_ref, own_in, dqt_ref, stat_ref, own_ref, dq_ref
):
    def put(rows, part):
        own_ref[rows, :] = own_in[rows, :] + part

    query, grad = operands(mine_ref, 1)
    dq_t = add_gradients(
        (mine_ref, e_ref, slope_ref, kt_ref),
        query, grad, stat_ref[0:1, :], stat_ref[1:2, :], put, dqt_ref[...],
    )
    dq_ref[...] = dq_rows(dq_t)


def call(kernel, arrays, outs, scratch=(), limit=8, aliases=None, space=pltpu.VMEM):
    return pl.pallas_call(
        kernel,
        in_specs=[pl.BlockSpec(memory_space=pltpu.VMEM)] * len(arrays),
        out_specs=[pl.BlockSpec(memory_space=pltpu.VMEM)] * len(outs),
        out_shape=[out if hasattr(out, "dtype") else pltpu.VMEM(*out) for out in outs],
        scratch_shapes=[pltpu.VMEM(*shape) for shape in scratch],
        input_output_aliases=aliases or {},
        compiler_params=pltpu.CompilerParams(vmem_limit_bytes=limit * 2**20),
    )(*(pltpu.with_memory_space_constraint(x, space) for x in arrays))


def pack_kernel(q_ref, k_ref, v_ref, g_ref, out_ref):
    for head in range(HEADS):
        columns = slice(head * HEAD_DIM, (head + 1) * HEAD_DIM)
        kv = jnp.concatenate([k_ref[:, columns], v_ref[:, columns]], axis=1)
        qg = jnp.concatenate([q_ref[:, columns], g_ref[:, columns]], axis=1)
        for ring in range(RINGS):
            out_ref[head * RINGS + ring, :BLOCK] = kv
            out_ref[head * RINGS + ring, BLOCK:] = qg[ring * SHARE : (ring + 1) * SHARE]


def pack(query, key, value, grad):
    shape = (RINGS * HEADS, BLOCK + SHARE, WIDE)
    return call(pack_kernel, (query, key, value, grad), [(shape, query.dtype)], space=pltpu.HBM)[0]


def unpack_kernel(in_ref, dq_ref, dk_ref, dv_ref):
    for pair in range(HEADS // 2):
        columns = slice(pair * WIDE, (pair + 1) * WIDE)
        sums = [0.0, 0.0]
        for ring in range(RINGS):
            one, two = (
                in_ref[(2 * pair + i) * RINGS + ring].astype(jnp.float32) for i in range(2)
            )
            sums = [sums[0] + one[:BLOCK], sums[1] + two[:BLOCK]]
            dq_ref[ring * SHARE : (ring + 1) * SHARE, columns] = jnp.concatenate(
                [one[BLOCK:, :HEAD_DIM], two[BLOCK:, :HEAD_DIM]], axis=1
            )
        one, two = sums
        dk_ref[:, columns] = jnp.concatenate([one[:, :HEAD_DIM], two[:, :HEAD_DIM]], axis=1)
        dv_ref[:, columns] = jnp.concatenate([one[:, HEAD_DIM:], two[:, HEAD_DIM:]], axis=1)


def unpack(parts):
    out = jax.ShapeDtypeStruct((BLOCK, HEADS * HEAD_DIM), jnp.float32)
    return call(unpack_kernel, (parts,), [out] * 3)


def combine_kernel(own_ref, other_ref, dq0_ref, dq1_ref, out_ref):
    total = own_ref[...] + other_ref[...].astype(jnp.float32)
    out_ref[:, :BLOCK] = total.astype(out_ref.dtype).reshape(-1, BLOCK, WIDE)
    each = dq0_ref.shape[0]
    out_ref[:each, BLOCK:] = dq0_ref[...]
    out_ref[each:, BLOCK:] = dq1_ref[...]


def per_device(query_proj, key_proj, value_proj, grad_attn):
    low, full = jnp.bfloat16, jnp.float32

    def spread(packed):
        return lax.all_to_all(packed, CHIPS, 0, 0, tiled=True)

    def swap(values):
        return lax.ppermute(values, "core", [(0, 1), (1, 0)])

    mine = spread(pack(query_proj, key_proj, value_proj, grad_attn))
    half = mine.shape[0] * BLOCK
    wide = ((half, QUERY_BLOCK), full)
    turned = ((HEAD_DIM, half), low)
    total = ((half, WIDE), full)
    dq_shape = ((QUERY_BLOCK // SHARE, SHARE, WIDE), low)
    dqt = ((HEAD_DIM, QUERY_BLOCK), full)
    eight = ((8, QUERY_BLOCK), full)
    pair = swap(mine)
    e, slope, kt, first = call(start_kernel, (mine,), [wide, wide, turned, eight])
    e, slope, other, own, dq0, dq_t, stats = call(
        main_kernel,
        (mine, pair, e, slope, kt, first),
        [wide, wide, ((half, WIDE), low), total, dq_shape, dqt, eight],
        scratch=[wide, wide, turned, total],
        limit=22,
        aliases={2: 0, 3: 1},
    )
    other = swap(other)
    own, dq1 = call(
        end_kernel, (mine, e, slope, kt, own, dq_t, stats), [total, dq_shape], aliases={4: 0}
    )
    back = call(combine_kernel, (own, other, dq0, dq1), [(mine.shape, low)])[0]
    return tuple(unpack(spread(back)))


def solution(mesh):
    fine = Mesh(
        mesh.devices.reshape(RINGS, 2, 4, 2, 2), ("y", "xh", "z", "xl", "core")
    )
    queries = P(("y", "xh", "z", "xl", "core"), None)
    tokens = P(("z", "xl", "core", "y", "xh"), None)
    return jax.shard_map(
        per_device,
        mesh=fine,
        in_specs=(queries, tokens, tokens, queries),
        out_specs=(queries, tokens, tokens),
        check_vma=False,
    )
```

```python
import jax
import jax.numpy as jnp
from jax import lax
from jax.experimental import pallas as pl
from jax.experimental.pallas import tpu as pltpu
from jax.sharding import Mesh, PartitionSpec as P

HEADS = 16
HEAD_DIM = 64
WIDE = 2 * HEAD_DIM
LOG2E = 1.4426950408889634
NN = (((1,), (0,)), ((), ()))
CHIPS = ("xl", "xh", "z", "y")
RINGS = 4
BLOCK = 64
SHARE = BLOCK // RINGS
QUERY_BLOCK = 512
GROUP = 2048
LONG = 4096
STEP = 512


def dot(left, right):
    return lax.dot_general(left, right, NN, preferred_element_type=jnp.float32)


def fold(values, op):
    return op(values.reshape(values.shape[0] // 8, 8, values.shape[1]), axis=0)


def over_rows(start, rows, step, unroll, body, carry):
    def iteration(i, carry):
        for j in range(unroll // step):
            carry = body(pl.multiple_of(start + i * unroll + j * step, step), carry)
        return carry

    return lax.fori_loop(0, rows // unroll, iteration, carry)


def operands(mine_ref, block):
    each = QUERY_BLOCK // SHARE
    qg = mine_ref[block * each : (block + 1) * each, BLOCK:, :].reshape(QUERY_BLOCK, WIDE)
    lane = lax.broadcasted_iota(jnp.int32, qg.shape, 1)
    zero = jnp.zeros_like(qg)
    query = jnp.where(lane < HEAD_DIM, qg * jnp.bfloat16(HEAD_DIM**-0.5), zero)
    return query, jnp.where(lane < HEAD_DIM, zero, qg)


def tokens_at(ref, first):
    return ref[pl.ds(first // BLOCK, STEP // BLOCK), :BLOCK, :].reshape(STEP, WIDE)


def add_scores(half, query_t, peak, keep_turned):
    kv_ref, e_ref, _, kt_ref = half

    def body(first, peak):
        kv = tokens_at(kv_ref, first)
        rows = pl.ds(first, STEP)
        scores = dot(kv, query_t) * LOG2E
        e_ref[rows, :] = scores
        if keep_turned:
            kt_ref[:, rows] = kv.T[:HEAD_DIM]
        return jnp.maximum(peak, fold(scores, jnp.max))

    rows = e_ref.shape[0]
    return over_rows(0, rows, STEP, rows, body, peak)


def add_sums(half, grad_t, peak, sums):
    kv_ref, e_ref, slope_ref, _ = half

    def body(first, carry):
        total, delta = carry
        rows = pl.ds(first, STEP)
        slopes = dot(tokens_at(kv_ref, first), grad_t)
        slope_ref[rows, :] = slopes
        e = jnp.exp2(e_ref[rows, :] - peak)
        e_ref[rows, :] = e
        return total + fold(e, jnp.sum), delta + fold(e * slopes, jnp.sum)

    return over_rows(0, e_ref.shape[0], STEP, LONG, body, sums)


def add_gradients(half, query, grad, factor, delta, put, dq_t):
    _, e_ref, slope_ref, kt_ref = half
    both = jnp.concatenate([query, grad], axis=0)

    def body(first, dq_t):
        rows = pl.ds(first, 256)
        probs = e_ref[rows, :] * factor
        weights = (probs * (slope_ref[rows, :] - delta)).astype(jnp.bfloat16)
        pair = jnp.concatenate([weights, probs.astype(jnp.bfloat16)], axis=1)
        put(rows, dot(pair, both))
        return dq_t + dot(kt_ref[:, rows], weights)

    return over_rows(0, e_ref.shape[0], 256, GROUP, body, dq_t)


def dq_rows(dq_t):
    dq = (dq_t * HEAD_DIM**-0.5).T.reshape(QUERY_BLOCK // SHARE, SHARE, HEAD_DIM)
    return jnp.concatenate([dq[:, : SHARE // 2], dq[:, SHARE // 2 :]], axis=2)


NONE = float("-inf")


def half_sums(half, query_t, grad_t, keep_turned=False):
    count = query_t.shape[1]
    none = jnp.zeros((8, count), jnp.float32)
    peak = add_scores(half, query_t, jnp.full((8, count), NONE), keep_turned)
    peak = jnp.max(peak, axis=0, keepdims=True)
    sums = add_sums(half, grad_t, peak, (none, none))
    return (peak, *(jnp.sum(x, axis=0, keepdims=True) for x in sums))


def joined(one, two):
    peak = jnp.maximum(one[0], two[0])
    first, second = jnp.exp2(one[0] - peak), jnp.exp2(two[0] - peak)
    inverse = 1.0 / (one[1] * first + two[1] * second)
    delta = (one[2] * first + two[2] * second) * inverse
    return first * inverse, second * inverse, delta


def start_kernel(mine_ref, e_ref, slope_ref, kt_ref, stat_ref):
    query, grad = operands(mine_ref, 0)
    half = (mine_ref, e_ref, slope_ref, kt_ref)
    for i, row in enumerate(half_sums(half, query.T, grad.T, keep_turned=True)):
        stat_ref[i : i + 1, :] = row


def main_kernel(
    mine_ref, pair_ref, e_in, slope_in, kt_ref, first_ref,
    e_ref, slope_ref, other_ref, own_ref, dq_ref, dqt_ref, stat_ref,
    e_pair, slope_pair, kt_pair, sum_pair,
):
    del e_in, slope_in
    mine = (mine_ref, e_ref, slope_ref, kt_ref)
    pair = (pair_ref, e_pair, slope_pair, kt_pair)

    query, grad = operands(mine_ref, 0)
    own_sums = tuple(first_ref[i : i + 1, :] for i in range(3))
    pair_sums = half_sums(pair, query.T, grad.T, keep_turned=True)
    own_factor, pair_factor, delta = joined(own_sums, pair_sums)

    def put_own(rows, part):
        own_ref[rows, :] = part

    def put_pair(rows, part):
        sum_pair[rows, :] = part

    dq_t = jnp.zeros(dqt_ref.shape, jnp.float32)
    dq_t = add_gradients(mine, query, grad, own_factor, delta, put_own, dq_t)
    dq_t = add_gradients(pair, query, grad, pair_factor, delta, put_pair, dq_t)
    dq_ref[...] = dq_rows(dq_t)

    query, grad = operands(mine_ref, 1)
    query_t, grad_t = query.T, grad.T
    own_sums = half_sums(mine, query_t, grad_t)
    pair_sums = half_sums(pair, query_t, grad_t)
    own_factor, pair_factor, delta = joined(own_sums, pair_sums)

    def put_other(rows, part):
        other_ref[rows, :] = (sum_pair[rows, :] + part).astype(other_ref.dtype)

    dqt_ref[...] = add_gradients(
        pair, query, grad, pair_factor, delta, put_other, jnp.zeros(dqt_ref.shape, jnp.float32)
    )
    stat_ref[0:1, :] = own_factor
    stat_ref[1:2, :] = delta


def end_kernel(
    mine_ref, e_ref, slope_ref, kt_ref, own_in, dqt_ref, stat_ref, own_ref, dq_ref
):
    def put(rows, part):
        own_ref[rows, :] = own_in[rows, :] + part

    query, grad = operands(mine_ref, 1)
    dq_t = add_gradients(
        (mine_ref, e_ref, slope_ref, kt_ref),
        query, grad, stat_ref[0:1, :], stat_ref[1:2, :], put, dqt_ref[...],
    )
    dq_ref[...] = dq_rows(dq_t)


def call(kernel, arrays, outs, scratch=(), limit=8, aliases=None, space=pltpu.VMEM):
    return pl.pallas_call(
        kernel,
        in_specs=[pl.BlockSpec(memory_space=pltpu.VMEM)] * len(arrays),
        out_specs=[pl.BlockSpec(memory_space=pltpu.VMEM)] * len(outs),
        out_shape=[out if hasattr(out, "dtype") else pltpu.VMEM(*out) for out in outs],
        scratch_shapes=[pltpu.VMEM(*shape) for shape in scratch],
        input_output_aliases=aliases or {},
        compiler_params=pltpu.CompilerParams(vmem_limit_bytes=limit * 2**20),
    )(*(pltpu.with_memory_space_constraint(x, space) for x in arrays))


def pack_kernel(q_ref, k_ref, v_ref, g_ref, out_ref):
    for head in range(HEADS):
        columns = slice(head * HEAD_DIM, (head + 1) * HEAD_DIM)
        kv = jnp.concatenate([k_ref[:, columns], v_ref[:, columns]], axis=1)
        qg = jnp.concatenate([q_ref[:, columns], g_ref[:, columns]], axis=1)
        for ring in range(RINGS):
            out_ref[head * RINGS + ring, :BLOCK] = kv
            out_ref[head * RINGS + ring, BLOCK:] = qg[ring * SHARE : (ring + 1) * SHARE]


def pack(query, key, value, grad):
    shape = (RINGS * HEADS, BLOCK + SHARE, WIDE)
    return call(pack_kernel, (query, key, value, grad), [(shape, query.dtype)], space=pltpu.HBM)[0]


def unpack_kernel(in_ref, dq_ref, dk_ref, dv_ref):
    each = in_ref.shape[1] // 2
    for pair in range(HEADS // 2):
        columns = slice(pair * WIDE, (pair + 1) * WIDE)
        sums = [0.0, 0.0]
        for twice in range(RINGS // 2):
            found = [
                in_ref[(2 * pair + i) * RINGS // 2 + twice].astype(jnp.float32) for i in range(2)
            ]
            for j in range(2):
                one, two = (x[j * each : (j + 1) * each] for x in found)
                sums = [sums[0] + one[:BLOCK], sums[1] + two[:BLOCK]]
                one, two = one[BLOCK:], two[BLOCK:]
                first = (2 * twice + j) * SHARE
                dq_ref[first : first + SHARE // 2, columns] = jnp.concatenate(
                    [one[:, :HEAD_DIM], two[:, :HEAD_DIM]], axis=1
                )
                dq_ref[first + SHARE // 2 : first + SHARE, columns] = jnp.concatenate(
                    [one[:, HEAD_DIM:], two[:, HEAD_DIM:]], axis=1
                )
        one, two = sums
        dk_ref[:, columns] = jnp.concatenate([one[:, :HEAD_DIM], two[:, :HEAD_DIM]], axis=1)
        dv_ref[:, columns] = jnp.concatenate([one[:, HEAD_DIM:], two[:, HEAD_DIM:]], axis=1)


def unpack(parts):
    out = jax.ShapeDtypeStruct((BLOCK, HEADS * HEAD_DIM), jnp.float32)
    return call(unpack_kernel, (parts,), [out] * 3)


def combine_kernel(own_ref, other_ref, dq0_ref, dq1_ref, out_ref):
    total = own_ref[...] + other_ref[...].astype(jnp.float32)
    total = total.reshape(-1, 2, BLOCK, WIDE)
    each = dq0_ref.shape[0] // 2
    for ref, first in ((dq0_ref, 0), (dq1_ref, each)):
        here = total[first : first + each]
        dq = ref[...].reshape(each, 2, SHARE // 2, WIDE)
        rows = [here[:, 0], dq[:, 0], here[:, 1], dq[:, 1]]
        out_ref[first : first + each] = jnp.concatenate(rows, axis=1).astype(out_ref.dtype)


def per_device(query_proj, key_proj, value_proj, grad_attn):
    low, full = jnp.bfloat16, jnp.float32

    def spread(packed):
        return lax.all_to_all(packed, CHIPS, 0, 0, tiled=True)

    def swap(values):
        return lax.ppermute(values, "core", [(0, 1), (1, 0)])

    mine = spread(pack(query_proj, key_proj, value_proj, grad_attn))
    half = mine.shape[0] * BLOCK
    wide = ((half, QUERY_BLOCK), full)
    turned = ((HEAD_DIM, half), low)
    total = ((half, WIDE), full)
    dq_shape = ((QUERY_BLOCK // SHARE, SHARE // 2, WIDE), full)
    dqt = ((HEAD_DIM, QUERY_BLOCK), full)
    eight = ((8, QUERY_BLOCK), full)
    pair = swap(mine)
    e, slope, kt, first = call(start_kernel, (mine,), [wide, wide, turned, eight])
    e, slope, other, own, dq0, dq_t, stats = call(
        main_kernel,
        (mine, pair, e, slope, kt, first),
        [wide, wide, ((half, WIDE), low), total, dq_shape, dqt, eight],
        scratch=[wide, wide, turned, total],
        limit=22,
        aliases={2: 0, 3: 1},
    )
    other = swap(other)
    own, dq1 = call(
        end_kernel, (mine, e, slope, kt, own, dq_t, stats), [total, dq_shape], aliases={4: 0}
    )
    sources, each = mine.shape[0], BLOCK + SHARE // 2
    shape = (sources // 2, 2 * each, WIDE)
    back = call(combine_kernel, (own, other, dq0, dq1), [(shape, low)])[0]
    back = spread(back.reshape(sources, each, WIDE))
    return tuple(unpack(back.reshape(shape)))


def solution(mesh):
    fine = Mesh(
        mesh.devices.reshape(RINGS, 2, 4, 2, 2), ("y", "xh", "z", "xl", "core")
    )
    queries = P(("y", "xh", "z", "xl", "core"), None)
    tokens = P(("z", "xl", "core", "y", "xh"), None)
    return jax.shard_map(
        per_device,
        mesh=fine,
        in_specs=(queries, tokens, tokens, queries),
        out_specs=(queries, tokens, tokens),
        check_vma=False,
    )
```

```python
import jax
import jax.numpy as jnp
from jax import lax
from jax.experimental import pallas as pl
from jax.experimental.pallas import tpu as pltpu
from jax.sharding import Mesh, PartitionSpec as P

HEADS = 16
HEAD_DIM = 64
WIDE = 2 * HEAD_DIM
LOG2E = 1.4426950408889634
NN = (((1,), (0,)), ((), ()))
CHIPS = ("xl", "xh", "z", "y")
RINGS = 4
BLOCK = 64
SHARE = BLOCK // RINGS
QUERY_BLOCK = 512
GROUP = 2048
LONG = 4096
STEP = 512


def dot(left, right):
    return lax.dot_general(left, right, NN, preferred_element_type=jnp.float32)


def fold(values, op):
    return op(values.reshape(values.shape[0] // 8, 8, values.shape[1]), axis=0)


def over_rows(start, rows, step, unroll, body, carry):
    def iteration(i, carry):
        for j in range(unroll // step):
            carry = body(pl.multiple_of(start + i * unroll + j * step, step), carry)
        return carry

    return lax.fori_loop(0, rows // unroll, iteration, carry)


def operands(mine_ref, block):
    each = QUERY_BLOCK // SHARE
    qg = mine_ref[block * each : (block + 1) * each, BLOCK:, :].reshape(QUERY_BLOCK, WIDE)
    lane = lax.broadcasted_iota(jnp.int32, qg.shape, 1)
    zero = jnp.zeros_like(qg)
    query = jnp.where(lane < HEAD_DIM, qg * jnp.bfloat16(HEAD_DIM**-0.5), zero)
    return query, jnp.where(lane < HEAD_DIM, zero, qg)


def tokens_at(ref, first):
    return ref[pl.ds(first // BLOCK, STEP // BLOCK), :BLOCK, :].reshape(STEP, WIDE)


def add_scores(half, query_t, peak, keep_turned):
    kv_ref, e_ref, _, kt_ref = half

    def body(first, peak):
        kv = tokens_at(kv_ref, first)
        rows = pl.ds(first, STEP)
        scores = dot(kv, query_t) * LOG2E
        e_ref[rows, :] = scores
        if keep_turned:
            kt_ref[:, rows] = kv.T[:HEAD_DIM]
        return jnp.maximum(peak, fold(scores, jnp.max))

    rows = e_ref.shape[0]
    return over_rows(0, rows, STEP, rows, body, peak)


def add_sums(half, grad_t, peak, sums):
    kv_ref, e_ref, slope_ref, _ = half

    def body(first, carry):
        total, delta = carry
        rows = pl.ds(first, STEP)
        slopes = dot(tokens_at(kv_ref, first), grad_t)
        slope_ref[rows, :] = slopes
        e = jnp.exp2(e_ref[rows, :] - peak)
        e_ref[rows, :] = e
        return total + fold(e, jnp.sum), delta + fold(e * slopes, jnp.sum)

    return over_rows(0, e_ref.shape[0], STEP, LONG, body, sums)


def add_gradients(half, query, grad, factor, delta, put, dq_t, unroll=GROUP):
    _, e_ref, slope_ref, kt_ref = half
    parts = [slice(i, i + QUERY_BLOCK // 2) for i in (0, QUERY_BLOCK // 2)]
    both = jnp.concatenate([x[part] for part in parts for x in (query, grad)], axis=0)

    def body(first, dq_t):
        rows = pl.ds(first, 256)
        probs = e_ref[rows, :] * factor
        weights = (probs * (slope_ref[rows, :] - delta)).astype(jnp.bfloat16)
        low = probs.astype(jnp.bfloat16)
        pair = [x[:, part] for part in parts for x in (weights, low)]
        put(rows, dot(jnp.concatenate(pair, axis=1), both))
        return dq_t + dot(kt_ref[:, rows], weights)

    return over_rows(0, e_ref.shape[0], 256, unroll, body, dq_t)


def dq_rows(dq_t):
    dq = (dq_t * HEAD_DIM**-0.5).T.reshape(QUERY_BLOCK // SHARE, SHARE, HEAD_DIM)
    return jnp.concatenate([dq[:, : SHARE // 2], dq[:, SHARE // 2 :]], axis=2)


NONE = float("-inf")


def half_sums(half, query_t, grad_t, keep_turned=False):
    count = query_t.shape[1]
    none = jnp.zeros((8, count), jnp.float32)
    peak = add_scores(half, query_t, jnp.full((8, count), NONE), keep_turned)
    peak = jnp.max(peak, axis=0, keepdims=True)
    sums = add_sums(half, grad_t, peak, (none, none))
    return (peak, *(jnp.sum(x, axis=0, keepdims=True) for x in sums))


def joined(one, two):
    peak = jnp.maximum(one[0], two[0])
    first, second = jnp.exp2(one[0] - peak), jnp.exp2(two[0] - peak)
    inverse = 1.0 / (one[1] * first + two[1] * second)
    delta = (one[2] * first + two[2] * second) * inverse
    return first * inverse, second * inverse, delta


def start_kernel(mine_ref, e_ref, slope_ref, kt_ref, stat_ref):
    query, grad = operands(mine_ref, 0)
    half = (mine_ref, e_ref, slope_ref, kt_ref)
    for i, row in enumerate(half_sums(half, query.T, grad.T, keep_turned=True)):
        stat_ref[i : i + 1, :] = row


def main_kernel(
    mine_ref, pair_ref, e_in, slope_in, kt_ref, first_ref,
    e_ref, slope_ref, other_ref, own_ref, dq_ref, dqt_ref, stat_ref,
    e_pair, slope_pair, kt_pair, sum_pair,
):
    del e_in, slope_in
    mine = (mine_ref, e_ref, slope_ref, kt_ref)
    pair = (pair_ref, e_pair, slope_pair, kt_pair)

    query, grad = operands(mine_ref, 0)
    own_sums = tuple(first_ref[i : i + 1, :] for i in range(3))
    pair_sums = half_sums(pair, query.T, grad.T, keep_turned=True)
    own_factor, pair_factor, delta = joined(own_sums, pair_sums)

    def put_own(rows, part):
        own_ref[rows, :] = part

    def put_pair(rows, part):
        sum_pair[rows, :] = part

    dq_t = jnp.zeros(dqt_ref.shape, jnp.float32)
    dq_t = add_gradients(mine, query, grad, own_factor, delta, put_own, dq_t)
    dq_t = add_gradients(pair, query, grad, pair_factor, delta, put_pair, dq_t)
    dq_ref[...] = dq_rows(dq_t)

    query, grad = operands(mine_ref, 1)
    query_t, grad_t = query.T, grad.T
    own_sums = half_sums(mine, query_t, grad_t)
    pair_sums = half_sums(pair, query_t, grad_t)
    own_factor, pair_factor, delta = joined(own_sums, pair_sums)

    def put_other(rows, part):
        other_ref[rows, :] = (sum_pair[rows, :] + part).astype(other_ref.dtype)

    dqt_ref[...] = add_gradients(
        pair, query, grad, pair_factor, delta, put_other, jnp.zeros(dqt_ref.shape, jnp.float32)
    )
    stat_ref[0:1, :] = own_factor
    stat_ref[1:2, :] = delta


def end_kernel(
    mine_ref, e_ref, slope_ref, kt_ref, own_in, dqt_ref, stat_ref, own_ref, dq_ref
):
    def put(rows, part):
        own_ref[rows, :] = own_in[rows, :] + part

    query, grad = operands(mine_ref, 1)
    dq_t = add_gradients(
        (mine_ref, e_ref, slope_ref, kt_ref),
        query, grad, stat_ref[0:1, :], stat_ref[1:2, :], put, dqt_ref[...], LONG,
    )
    dq_ref[...] = dq_rows(dq_t)


def call(kernel, arrays, outs, scratch=(), limit=8, aliases=None, space=pltpu.VMEM):
    return pl.pallas_call(
        kernel,
        in_specs=[pl.BlockSpec(memory_space=pltpu.VMEM)] * len(arrays),
        out_specs=[pl.BlockSpec(memory_space=pltpu.VMEM)] * len(outs),
        out_shape=[out if hasattr(out, "dtype") else pltpu.VMEM(*out) for out in outs],
        scratch_shapes=[pltpu.VMEM(*shape) for shape in scratch],
        input_output_aliases=aliases or {},
        compiler_params=pltpu.CompilerParams(vmem_limit_bytes=limit * 2**20),
    )(*(pltpu.with_memory_space_constraint(x, space) for x in arrays))


def pack_kernel(q_ref, k_ref, v_ref, g_ref, out_ref):
    for head in range(HEADS):
        columns = slice(head * HEAD_DIM, (head + 1) * HEAD_DIM)
        kv = jnp.concatenate([k_ref[:, columns], v_ref[:, columns]], axis=1)
        qg = jnp.concatenate([q_ref[:, columns], g_ref[:, columns]], axis=1)
        for ring in range(RINGS):
            out_ref[head * RINGS + ring, :BLOCK] = kv
            out_ref[head * RINGS + ring, BLOCK:] = qg[ring * SHARE : (ring + 1) * SHARE]


def pack(query, key, value, grad):
    shape = (RINGS * HEADS, BLOCK + SHARE, WIDE)
    return call(pack_kernel, (query, key, value, grad), [(shape, query.dtype)], space=pltpu.HBM)[0]


def unpack_kernel(in_ref, dq_ref, dk_ref, dv_ref):
    each = in_ref.shape[1] // 2
    for pair in range(HEADS // 2):
        columns = slice(pair * WIDE, (pair + 1) * WIDE)
        sums = [0.0, 0.0]
        for twice in range(RINGS // 2):
            found = [
                in_ref[(2 * pair + i) * RINGS // 2 + twice].astype(jnp.float32) for i in range(2)
            ]
            for j in range(2):
                one, two = (x[j * each : (j + 1) * each] for x in found)
                sums = [sums[0] + one[:BLOCK], sums[1] + two[:BLOCK]]
                one, two = one[BLOCK:], two[BLOCK:]
                first = (2 * twice + j) * SHARE
                dq_ref[first : first + SHARE // 2, columns] = jnp.concatenate(
                    [one[:, :HEAD_DIM], two[:, :HEAD_DIM]], axis=1
                )
                dq_ref[first + SHARE // 2 : first + SHARE, columns] = jnp.concatenate(
                    [one[:, HEAD_DIM:], two[:, HEAD_DIM:]], axis=1
                )
        one, two = sums
        dk_ref[:, columns] = jnp.concatenate([one[:, :HEAD_DIM], two[:, :HEAD_DIM]], axis=1)
        dv_ref[:, columns] = jnp.concatenate([one[:, HEAD_DIM:], two[:, HEAD_DIM:]], axis=1)


def unpack(parts):
    out = jax.ShapeDtypeStruct((BLOCK, HEADS * HEAD_DIM), jnp.float32)
    return call(unpack_kernel, (parts,), [out] * 3)


def combine_kernel(own_ref, other_ref, dq0_ref, dq1_ref, out_ref):
    total = own_ref[...] + other_ref[...].astype(jnp.float32)
    total = total.reshape(-1, 2, BLOCK, WIDE)
    each = dq0_ref.shape[0] // 2
    for ref, first in ((dq0_ref, 0), (dq1_ref, each)):
        here = total[first : first + each]
        dq = ref[...].reshape(each, 2, SHARE // 2, WIDE)
        rows = [here[:, 0], dq[:, 0], here[:, 1], dq[:, 1]]
        out_ref[first : first + each] = jnp.concatenate(rows, axis=1).astype(out_ref.dtype)


def per_device(query_proj, key_proj, value_proj, grad_attn):
    low, full = jnp.bfloat16, jnp.float32

    def spread(packed):
        return lax.all_to_all(packed, CHIPS, 0, 0, tiled=True)

    def swap(values):
        return lax.ppermute(values, "core", [(0, 1), (1, 0)])

    mine = spread(pack(query_proj, key_proj, value_proj, grad_attn))
    half = mine.shape[0] * BLOCK
    wide = ((half, QUERY_BLOCK), full)
    turned = ((HEAD_DIM, half), low)
    total = ((half, WIDE), full)
    dq_shape = ((QUERY_BLOCK // SHARE, SHARE // 2, WIDE), full)
    dqt = ((HEAD_DIM, QUERY_BLOCK), full)
    eight = ((8, QUERY_BLOCK), full)
    pair = swap(mine)
    e, slope, kt, first = call(start_kernel, (mine,), [wide, wide, turned, eight])
    e, slope, other, own, dq0, dq_t, stats = call(
        main_kernel,
        (mine, pair, e, slope, kt, first),
        [wide, wide, ((half, WIDE), low), total, dq_shape, dqt, eight],
        scratch=[wide, wide, turned, total],
        limit=22,
        aliases={2: 0, 3: 1},
    )
    other = swap(other)
    own, dq1 = call(
        end_kernel, (mine, e, slope, kt, own, dq_t, stats), [total, dq_shape], aliases={4: 0}
    )
    sources, each = mine.shape[0], BLOCK + SHARE // 2
    shape = (sources // 2, 2 * each, WIDE)
    back = call(combine_kernel, (own, other, dq0, dq1), [(shape, low)])[0]
    back = spread(back.reshape(sources, each, WIDE))
    return tuple(unpack(back.reshape(shape)))


def solution(mesh):
    fine = Mesh(
        mesh.devices.reshape(RINGS, 2, 4, 2, 2), ("y", "xh", "z", "xl", "core")
    )
    queries = P(("y", "xh", "z", "xl", "core"), None)
    tokens = P(("z", "xl", "core", "y", "xh"), None)
    return jax.shard_map(
        per_device,
        mesh=fine,
        in_specs=(queries, tokens, tokens, queries),
        out_specs=(queries, tokens, tokens),
        check_vma=False,
    )
```
